32 devices in a mesh: dp: 8 (over y, x, core), tensor: 4 (over z).
Axes of the slice: x: 2, y: 2, z: 4, core: 2. Of those that a mesh axis runs over, the one named last changes fastest.
Arguments:
- tokens: bfloat16 [4096, 768], P('dp'), may hold values from -6 to 6
- encoded: bfloat16 [16384, 768], P('dp'), may hold values from -6 to 6
- cotangent: bfloat16 [4096, 768], P('dp'), may hold values from -6 to 6
- seq_lengths: int32 [32], P('dp'), may hold values from 32 to 256, as said below
- enc_slot: int32 [32], P('dp'), may hold values from 0 to 3, as said below
- buckets: int32 [256], replicated, may hold values from 0 to 31, as said below
- gain_self: float32 [768], replicated, may hold values from 0.25 to 1.75
- gain_cross: float32 [768], replicated, may hold values from 0.25 to 1.75
- gain_ffn: float32 [768], replicated, may hold values from 0.25 to 1.75
- self_query: bfloat16 [768, 768], P(None, 'tensor'), may hold values from -0.02734375 to 0.02734375
- self_key: bfloat16 [768, 768], P(None, 'tensor'), may hold values from -0.21875 to 0.21875
- self_value: bfloat16 [768, 768], P(None, 'tensor'), may hold values from -0.21875 to 0.21875
- self_out: bfloat16 [768, 768], P('tensor'), may hold values from -1.75 to 1.75
- bias_table: bfloat16 [32, 12], P(None, 'tensor'), may hold values from -4 to 4
- cross_query: bfloat16 [768, 768], P(None, 'tensor'), may hold values from -0.02734375 to 0.02734375
- cross_key: bfloat16 [768, 768], P(None, 'tensor'), may hold values from -0.21875 to 0.21875
- cross_value: bfloat16 [768, 768], P(None, 'tensor'), may hold values from -0.21875 to 0.21875
- cross_out: bfloat16 [768, 768], P('tensor'), may hold values from -3.5 to 3.5
- gate_weight: bfloat16 [768, 2048], P(None, 'tensor'), may hold values from -0.21875 to 0.21875
- up_weight: bfloat16 [768, 2048], P(None, 'tensor'), may hold values from -0.21875 to 0.21875
- down_weight: bfloat16 [2048, 768], P('tensor'), may hold values from -0.25 to 0.25
Outputs:
- layer_out: bfloat16 [4096, 768], P('dp')
- grad_tokens: float32 [4096, 768], P('dp')
- grad_encoded: float32 [16384, 768], P('dp', 'tensor')
- grad_gain_self: float32 [768], replicated
- grad_gain_cross: float32 [768], replicated
- grad_gain_ffn: float32 [768], replicated
- grad_self_query: float32 [768, 768], P('dp', 'tensor')
- grad_self_key: float32 [768, 768], P('dp', 'tensor')
- grad_self_value: float32 [768, 768], P('dp', 'tensor')
- grad_self_out: float32 [768, 768], P('tensor', 'dp')
- grad_bias_table: float32 [32, 12], P(None, 'tensor')
- grad_cross_query: float32 [768, 768], P('dp', 'tensor')
- grad_cross_key: float32 [768, 768], P('dp', 'tensor')
- grad_cross_value: float32 [768, 768], P('dp', 'tensor')
- grad_cross_out: float32 [768, 768], P('tensor', 'dp')
- grad_gate_weight: float32 [768, 2048], P('dp', 'tensor')
- grad_up_weight: float32 [768, 2048], P('dp', 'tensor')
- grad_down_weight: float32 [2048, 768], P('tensor', 'dp')
The draws below stay inside these ranges and needn't reach their ends.
Inputs may be any that keep to these rules, and one draw needn't show every extreme that they name: `seq_lengths`: in each group of 4 entries the lengths sum to at most 512, and the sequences fill their group's rows from the first, in slot order; the rest is padding. In each group one sequence has 256 tokens and another 256 // 8. `enc_slot`: each group of 4 entries is a permutation of 0 to 3. buckets[d] = d for d < 16, never falls as d grows, and is 31 at d = 255.
All inputs are finite; a program needn't handle non-finite values.
Results may differ from the reference program's by a relative error of at most 0.025.
Values may be sent and summed in bfloat16 or wider, within the bound.
A program may use at most 256 MiB of HBM per device.

```python
from functools import partial
import jax
import jax.numpy as jnp
from jax import lax

D = 768
H = 12
HD = 64
FF = 2048
NB = 32
L = 256
SLOTS = 4
ROWS = 512
ENC = 512
TOKENS = 4096
ENC_ROWS = 16384
N_DP = 8


def draw_seq_lengths(key, part):
    key = jax.random.fold_in(key, 11)
    first_key, second_key, third_key = jax.random.split(key, 3)
    upper = min(L, (ROWS - L - L // 8) // (SLOTS - 2))
    lengths = jax.random.randint(first_key, (N_DP, SLOTS), L // 8, upper + 1)
    longest = jax.random.randint(second_key, (N_DP, 1), 0, SLOTS)
    shortest = (longest + 1 + jax.random.randint(third_key, (N_DP, 1), 0, SLOTS - 1)) % SLOTS
    where_at = jnp.arange(SLOTS)[None, :]
    lengths = jnp.where(where_at == longest, L, lengths)
    lengths = jnp.where(where_at == shortest, L // 8, lengths)
    return lengths.reshape(-1).astype(jnp.int32)


def draw_enc_slot(key, part):
    key = jax.random.fold_in(key, 23)
    scores = jax.random.randint(key, (N_DP, SLOTS), 0, 1 << 20) * SLOTS + jnp.arange(SLOTS, dtype=jnp.int32)[None, :]
    return jnp.argsort(scores, axis=1).reshape(-1).astype(jnp.int32)


def draw_buckets(key, part):
    key = jax.random.fold_in(key, 37)
    places = jax.random.permutation(key, L - NB // 2)[:NB // 2] + NB // 2
    distance = jnp.arange(L, dtype=jnp.int32)
    later_bucket = jnp.sum((places[None, :] <= distance[:, None]).astype(jnp.int32), axis=1) + NB // 2 - 1
    return jnp.where(distance < NB // 2, distance, later_bucket).astype(jnp.int32)


def levels(stream_key, dims, cuts, smallest, high):
    loudness = 1.0
    for position, blocks in cuts:
        draws = jax.random.uniform(jax.random.fold_in(jax.random.fold_in(stream_key, 6), position), (blocks,), jnp.float32, smallest / len(cuts), high / len(cuts))
        loudness = loudness * jnp.repeat(jnp.exp(draws), dims[position] // blocks).reshape((-1,) + (1,) * (len(dims) - 1 - position))
    return loudness


def noise(own_key, dims, width, bound, cuts=(), held_as=jnp.bfloat16):
    gain = levels(own_key, dims, cuts, -0.22, 0.18) if cuts else 1.0
    drawn = jax.random.normal(own_key, dims, jnp.float32) * width * gain
    return jnp.minimum(jnp.maximum(drawn, -bound), bound).astype(held_as)


def setup_inputs(seed: int = 0) -> dict:
    seeds = jax.random.split(jax.random.key(seed), 22)
    return {
        "tokens": noise(seeds[0], (TOKENS, D), 1.0, 6.0, ((0, 8),)),
        "encoded": noise(seeds[1], (ENC_ROWS, D), 1.0, 6.0, ((0, 8),)),
        "cotangent": noise(seeds[2], (TOKENS, D), 1.0, 6.0, ((0, 8),)),
        "seq_lengths": draw_seq_lengths(jax.random.fold_in(seeds[21], 71), 0),
        "enc_slot": draw_enc_slot(jax.random.fold_in(seeds[21], 71), 0),
        "buckets": draw_buckets(jax.random.fold_in(seeds[21], 71), 0),
        "gain_self": jnp.clip(1.0 + 0.15 * jax.random.normal(seeds[6], (D,), jnp.float32), 0.25, 1.75),
        "gain_cross": jnp.clip(1.0 + 0.15 * jax.random.normal(seeds[7], (D,), jnp.float32), 0.25, 1.75),
        "gain_ffn": jnp.clip(1.0 + 0.15 * jax.random.normal(seeds[8], (D,), jnp.float32), 0.25, 1.75),
        "self_query": noise(seeds[9], (D, H * HD), (D * HD) ** -0.5, 0.02734375, ((1, 4),)),
        "self_key": noise(seeds[10], (D, H * HD), D ** -0.5, 0.21875, ((1, 4),)),
        "self_value": noise(seeds[11], (D, H * HD), D ** -0.5, 0.21875, ((1, 4),)),
        "self_out": noise(seeds[12], (H * HD, D), (max(H * HD // 64, 1)) ** -0.5, 1.75, ((0, 4),)),
        "bias_table": noise(seeds[13], (NB, H), 1.0, 4.0, ((1, 4),)),
        "cross_query": noise(seeds[14], (D, H * HD), (D * HD) ** -0.5, 0.02734375, ((1, 4),)),
        "cross_key": noise(seeds[15], (D, H * HD), D ** -0.5, 0.21875, ((1, 4),)),
        "cross_value": noise(seeds[16], (D, H * HD), D ** -0.5, 0.21875, ((1, 4),)),
        "cross_out": noise(seeds[17], (H * HD, D), (max(H * HD // 256, 1)) ** -0.5, 3.5, ((0, 4),)),
        "gate_weight": noise(seeds[18], (D, FF), D ** -0.5, 0.21875, ((1, 4),)),
        "up_weight": noise(seeds[19], (D, FF), D ** -0.5, 0.21875, ((1, 4),)),
        "down_weight": noise(seeds[20], (FF, D), (FF // 4) ** -0.5, 0.25, ((0, 4),)),
    }


@jax.custom_vjp
def low(v):
    return lax.optimization_barrier(v.astype(jnp.bfloat16)).astype(jnp.float32)

@jax.custom_vjp
def low_back(v):
    return v

def low_keep(v):
    return (low(v), None)

def low_pass(kept, grad):
    return (grad,)

def back_keep(v):
    return (v, None)

def back_low(kept, grad):
    return (low(grad),)
low.defvjp(low_keep, low_pass)
low_back.defvjp(back_keep, back_low)
eps = 1e-06
masked_score = -1e+30
highest = lax.Precision.HIGHEST

def both_ways(operand):
    return low(low_back(operand))

def rms_norm(operand, gain_vector):
    return operand * lax.rsqrt(lax.optimization_barrier(jnp.mean(operand * operand, axis=-1, keepdims=True)) + eps) * gain_vector

def matmul(left_side, right_side):
    return jnp.dot(left_side, right_side, precision=highest, preferred_element_type=jnp.float32)

def heads_of(operand):
    return operand.reshape(operand.shape[0], -1, HD)

def layout(lengths, slots_of, row_count):
    seq_ends = jnp.cumsum(lengths).astype(jnp.int32)
    seq_starts = (seq_ends - lengths).astype(jnp.int32)
    where_row = jnp.arange(row_count, dtype=jnp.int32)
    segment = lax.optimization_barrier(jnp.sum((where_row[:, None] >= seq_ends[None, :]).astype(jnp.int32), axis=1))
    all_starts = jnp.concatenate([seq_starts, seq_ends[-1:]]).astype(jnp.int32)
    labels = jnp.arange(all_starts.shape[0], dtype=jnp.int32)
    chosen = segment[:, None] == labels[None, :]
    offset = where_row - lax.optimization_barrier(jnp.sum(jnp.where(chosen, all_starts[None, :], 0), axis=1)).astype(jnp.int32)
    slot_table = jnp.concatenate([slots_of.astype(jnp.int32), jnp.zeros((1,), jnp.int32)])
    row_slot = lax.optimization_barrier(jnp.sum(jnp.where(chosen, slot_table[None, :], 0), axis=1)).astype(jnp.int32)
    return (segment, offset, row_slot)

def softmax_rows(scores):
    row_max = lax.optimization_barrier(jnp.max(scores, axis=-1, keepdims=True))
    exp_scores = jnp.exp(scores - row_max)
    return exp_scores / lax.optimization_barrier(jnp.sum(exp_scores, axis=-1, keepdims=True))

def attend(query, key_rows, value_rows, extra, allowed):
    scores = jnp.einsum('ihd,jhd->hij', heads_of(query), heads_of(key_rows), precision=highest, preferred_element_type=jnp.float32) + extra
    scores = low_back(scores)
    scores = jnp.where(allowed[None], scores, masked_score)
    weights = low(softmax_rows(scores))
    result = jnp.einsum('hij,jhd->ihd', weights, heads_of(value_rows), precision=highest, preferred_element_type=jnp.float32)
    return both_ways(result.reshape(query.shape[0], -1))

def device_layer(weights, buckets, block_item):
    gain_self, gain_cross, gain_ffn, self_query, self_key, self_value, self_out, bias_table, cross_query, cross_key, cross_value, cross_out, gate_weight, up_weight, down_weight = weights
    hidden_in, enc_rows, segment, offset, row_slot = block_item
    last_distance = buckets.shape[0] - 1
    normed = low(rms_norm(hidden_in, gain_self))
    query = both_ways(matmul(normed, self_query))
    key_rows = both_ways(matmul(normed, self_key))
    value_rows = both_ways(matmul(normed, self_value))
    distance = jnp.clip(offset[:, None] - offset[None, :], 0, last_distance)
    rel_bias = jnp.moveaxis(bias_table[buckets[distance]], 2, 0)
    allowed = (segment[:, None] == segment[None, :]) & (offset[:, None] >= offset[None, :])
    attended = attend(query, key_rows, value_rows, rel_bias, allowed)
    after_self = hidden_in + low_back(matmul(attended, self_out))
    normed = low(rms_norm(after_self, gain_cross))
    query = both_ways(matmul(normed, cross_query))
    key_rows = both_ways(matmul(enc_rows, cross_key))
    value_rows = both_ways(matmul(enc_rows, cross_value))
    key_slot = jnp.arange(enc_rows.shape[0], dtype=jnp.int32) // ENC
    allowed = row_slot[:, None] == key_slot[None, :]
    attended = attend(query, key_rows, value_rows, jnp.zeros((), jnp.float32), allowed)
    after_cross = after_self + low_back(matmul(attended, cross_out))
    normed = low(rms_norm(after_cross, gain_ffn))
    gate_act = low_back(matmul(normed, gate_weight))
    up_act = low_back(matmul(normed, up_weight))
    inner_act = low(jax.nn.gelu(gate_act, approximate=True) * up_act)
    return after_cross + low_back(matmul(inner_act, down_weight))

def reference(tokens, encoded, cotangent, seq_lengths, enc_slot, buckets, gain_self, gain_cross, gain_ffn, self_query, self_key, self_value, self_out, bias_table, cross_query, cross_key, cross_value, cross_out, gate_weight, up_weight, down_weight):
    lengths = seq_lengths.reshape(N_DP, SLOTS)
    slot_rows = enc_slot.reshape(N_DP, SLOTS)
    segment, offset, row_slot = jax.vmap(partial(layout, row_count=ROWS))(lengths, slot_rows)
    live_rows = (segment < SLOTS).astype(jnp.float32).reshape(-1)
    floats = (tokens, encoded, gain_self, gain_cross, gain_ffn, self_query, self_key, self_value, self_out, bias_table, cross_query, cross_key, cross_value, cross_out, gate_weight, up_weight, down_weight)
    floats = tuple((operand.astype(jnp.float32) for operand in floats))

    def forward(token_floats, enc_floats, *weights):
        hidden_in = token_floats.reshape(N_DP, ROWS, D)
        enc_rows = enc_floats.reshape(N_DP, SLOTS * ENC, D)
        layer = jax.checkpoint(partial(device_layer, weights, buckets))
        outputs = lax.map(layer, (hidden_in, enc_rows, segment, offset, row_slot))
        return outputs.reshape(token_floats.shape)
    layer_out, pullback = jax.vjp(forward, *floats)
    grads = pullback(cotangent.astype(jnp.float32) * live_rows[:, None])
    layer_out = layer_out * live_rows[:, None]
    return (layer_out.astype(jnp.bfloat16), grads[0], grads[1], grads[2], grads[3], grads[4], grads[5], grads[6], grads[7], grads[8], grads[9], grads[10], grads[11], grads[12], grads[13], grads[14], grads[15], grads[16])
```

```python
from functools import partial

import jax
import jax.numpy as jnp
from jax import lax
from jax.experimental import pallas as pl
from jax.experimental.pallas import tpu as pltpu
from jax.sharding import PartitionSpec as P

HD = 64


eps = 1e-06
masked_score = -1e30
highest = lax.Precision.HIGHEST


def layout(lengths, slots_of, row_count):
    seq_ends = jnp.cumsum(lengths)
    seq_starts = seq_ends - lengths
    where_row = jnp.arange(row_count, dtype=jnp.int32)
    segment = jnp.sum((where_row[:, None] >= seq_ends[None, :]).astype(jnp.int32), axis=1)
    all_starts = jnp.concatenate([seq_starts, seq_ends[-1:]])
    labels = jnp.arange(all_starts.shape[0], dtype=jnp.int32)
    chosen = segment[:, None] == labels[None, :]
    offset = where_row - jnp.sum(jnp.where(chosen, all_starts[None, :], 0), axis=1)
    slot_table = jnp.concatenate([slots_of, jnp.zeros((1,), jnp.int32)])
    row_slot = jnp.sum(jnp.where(chosen, slot_table[None, :], 0), axis=1)
    return (segment, offset, row_slot)


def project(left_side, right_side):
    return jnp.dot(left_side, right_side, preferred_element_type=jnp.float32)


def contract_rows(left_side, right_side):
    return lax.dot_general(
        left_side, right_side, (((0,), (0,)), ((), ())), preferred_element_type=jnp.float32
    )


def contract_cols(left_side, right_side):
    return lax.dot_general(
        left_side, right_side, (((1,), (1,)), ((), ())), preferred_element_type=jnp.float32
    )


def norm_parts(operand):
    inverse = lax.rsqrt(jnp.mean(operand * operand, axis=-1, keepdims=True) + eps)
    return (operand * inverse, inverse)


def norm_back(grad_normed, gain_vector, scaled, inverse):
    grad_scaled = grad_normed * gain_vector
    return inverse * (grad_scaled - scaled * jnp.mean(grad_scaled * scaled, axis=-1, keepdims=True))


def glu_product(gate_act, up_act):
    return jax.nn.gelu(gate_act, approximate=True) * up_act


def dot_nn(left_side, right_side):
    return jnp.dot(left_side, right_side, preferred_element_type=jnp.float32)


def softmax_parts(scores):
    exp_scores = jnp.exp(scores - jnp.max(scores, axis=-1, keepdims=True))
    return exp_scores / jnp.sum(exp_scores, axis=-1, keepdims=True)


def self_weights(q_head, k_head, table_row, allowed):
    rows, cols = allowed.shape
    bias = pltpu.roll(
        jnp.broadcast_to(table_row, (rows, cols)), 0, 1, stride=1, stride_axis=0
    )
    scores = contract_cols(q_head, k_head) + bias
    return softmax_parts(jnp.where(allowed, scores, masked_score))


def self_allowed(seg_rows, seg_cols):
    shape = (seg_rows.shape[0], seg_cols.shape[1])
    row = lax.broadcasted_iota(jnp.int32, shape, 0)
    col = lax.broadcasted_iota(jnp.int32, shape, 1)
    return (seg_rows == seg_cols) & (col <= row)


def self_forward_kernel(q_ref, k_ref, v_ref, table_ref, seg_rows, seg_cols, out_ref):
    allowed = self_allowed(seg_rows[...], seg_cols[...])
    for head in range(q_ref.shape[1] // HD):
        lanes = slice(head * HD, (head + 1) * HD)
        weights = self_weights(
            q_ref[:, lanes], k_ref[:, lanes], table_ref[head : head + 1, :], allowed
        )
        out_ref[:, lanes] = dot_nn(weights.astype(jnp.bfloat16), v_ref[:, lanes]).astype(
            jnp.bfloat16
        )


def score_grads(weights, grad_weights):
    delta_rows = jnp.sum(weights * grad_weights, axis=-1, keepdims=True)
    return (weights * (grad_weights - delta_rows)).astype(jnp.bfloat16)


def self_backward_kernel(
    q_ref, k_ref, v_ref, table_ref, seg_rows, seg_cols, g_ref, dq_ref, dk_ref, dv_ref, skew_ref
):
    allowed = self_allowed(seg_rows[...], seg_cols[...])
    rows, cols = allowed.shape
    flip = (
        lax.broadcasted_iota(jnp.int32, (cols, cols), 0)
        + lax.broadcasted_iota(jnp.int32, (cols, cols), 1)
        == cols - 1
    ).astype(jnp.float32).astype(jnp.bfloat16)
    for head in range(q_ref.shape[1] // HD):
        lanes = slice(head * HD, (head + 1) * HD)
        q_head, k_head, v_head, g_head = (
            q_ref[:, lanes],
            k_ref[:, lanes],
            v_ref[:, lanes],
            g_ref[:, lanes],
        )
        weights = self_weights(q_head, k_head, table_ref[head : head + 1, :], allowed)
        grad_scores = score_grads(weights, contract_cols(g_head, v_head))
        dq_ref[:, lanes] = dot_nn(grad_scores, k_head).astype(jnp.bfloat16)
        dk_ref[:, lanes] = contract_rows(grad_scores, q_head).astype(jnp.bfloat16)
        dv_ref[:, lanes] = contract_rows(weights.astype(jnp.bfloat16), g_head).astype(
            jnp.bfloat16
        )
        skewed = pltpu.roll(dot_nn(grad_scores, flip), 0, 1, stride=1, stride_axis=0)
        skew_ref[head : head + 1, :] = jnp.sum(skewed, axis=0, keepdims=True)


def slot_masked(operand, slot_rows, slot):
    return jnp.where(slot_rows == slot, operand, jnp.zeros_like(operand))


def slot_cols(left_side, right_ref, lanes, slot_rows, slots):
    span = right_ref.shape[0] // slots
    return sum(
        contract_cols(
            slot_masked(left_side, slot_rows, slot),
            right_ref[slot * span : (slot + 1) * span, lanes],
        )
        for slot in range(slots)
    )


def slot_pick(left_side, right_ref, lanes, slot_rows, slots):
    span = right_ref.shape[0] // slots
    return sum(
        slot_masked(
            dot_nn(left_side, right_ref[slot * span : (slot + 1) * span, lanes]), slot_rows, slot
        )
        for slot in range(slots)
    )


def cross_forward_kernel(slots, q_ref, k_ref, v_ref, slot_ref, out_ref):
    slot_rows = slot_ref[...]
    for head in range(q_ref.shape[1] // HD):
        lanes = slice(head * HD, (head + 1) * HD)
        weights = softmax_parts(slot_cols(q_ref[:, lanes], k_ref, lanes, slot_rows, slots))
        out_ref[:, lanes] = slot_pick(
            weights.astype(jnp.bfloat16), v_ref, lanes, slot_rows, slots
        ).astype(jnp.bfloat16)


def cross_backward_kernel(
    slots, q_ref, k_ref, v_ref, slot_ref, g_ref, dq_ref, dk_ref, dv_ref
):
    slot_rows = slot_ref[...]
    span = k_ref.shape[0] // slots
    for head in range(q_ref.shape[1] // HD):
        lanes = slice(head * HD, (head + 1) * HD)
        q_head, g_head = q_ref[:, lanes], g_ref[:, lanes]
        weights = softmax_parts(slot_cols(q_head, k_ref, lanes, slot_rows, slots))
        grad_scores = score_grads(weights, slot_cols(g_head, v_ref, lanes, slot_rows, slots))
        weights_low = weights.astype(jnp.bfloat16)
        dq_ref[:, lanes] = slot_pick(grad_scores, k_ref, lanes, slot_rows, slots).astype(
            jnp.bfloat16
        )
        for slot in range(slots):
            keys = slice(slot * span, (slot + 1) * span)
            dk_ref[keys, lanes] = contract_rows(
                grad_scores, slot_masked(q_head, slot_rows, slot)
            ).astype(jnp.bfloat16)
            dv_ref[keys, lanes] = contract_rows(
                weights_low, slot_masked(g_head, slot_rows, slot)
            ).astype(jnp.bfloat16)


def run_kernel(body, outs, name, flops, *operands):
    whole = pl.BlockSpec(memory_space=pltpu.VMEM)
    return pl.pallas_call(
        body,
        out_shape=outs,
        in_specs=[whole] * len(operands),
        out_specs=jax.tree.map(lambda leaf: whole, outs),
        compiler_params=pltpu.CompilerParams(vmem_limit_bytes=48 * 1024 * 1024),
        cost_estimate=pl.CostEstimate(flops=flops, bytes_accessed=1 << 22, transcendentals=0),
        name=name,
    )(*operands)


def layer_pass(
    hidden_in,
    enc_rows,
    grad_layer,
    segment,
    row_slot,
    slots,
    buckets,
    weights,
    mixers,
    ffn_hook,
):
    (
        gain_self,
        gain_cross,
        gain_ffn,
        self_query,
        self_key,
        self_value,
        self_out,
        bias_table,
        cross_query,
        cross_key,
        cross_value,
        cross_out,
        gate_weight,
        up_weight,
        down_weight,
    ) = weights
    mix_self, mix_cross, mix_ffn, back_ffn, back_cross, back_self = mixers
    row_count = hidden_in.shape[0]
    span = buckets.shape[0]
    bias_values = bias_table.astype(jnp.float32)
    bucket_labels = jnp.arange(bias_values.shape[0], dtype=jnp.int32)
    bucket_onehot = (buckets[:, None] == bucket_labels[None, :]).astype(jnp.float32)
    distance_table = jnp.dot(
        bucket_onehot, bias_values, precision=highest, preferred_element_type=jnp.float32
    ).T
    back = lax.rem(row_count - jnp.arange(row_count, dtype=jnp.int32), row_count)
    skew_onehot = (back[:, None] == jnp.arange(span, dtype=jnp.int32)[None, :]).astype(jnp.float32)
    skew_table = jnp.dot(
        distance_table, skew_onehot.T, precision=highest, preferred_element_type=jnp.float32
    )
    seg_rows, seg_cols = segment[:, None], segment[None, :]
    slot_rows = row_slot[:, None]

    scaled_one, inverse_one = norm_parts(hidden_in)
    normed_one = (scaled_one * gain_self).astype(jnp.bfloat16)
    query_self = project(normed_one, self_query).astype(jnp.bfloat16)
    key_self = project(normed_one, self_key).astype(jnp.bfloat16)
    value_self = project(normed_one, self_value).astype(jnp.bfloat16)
    low_like = lambda operand: jax.ShapeDtypeStruct(operand.shape, jnp.bfloat16)
    pair_flops = 2 * row_count * row_count * self_query.shape[1]
    attended_self = run_kernel(
        self_forward_kernel,
        low_like(query_self),
        "self_forward",
        8 * pair_flops,
        query_self,
        key_self,
        value_self,
        skew_table,
        seg_rows,
        seg_cols,
    )
    after_self = hidden_in + mix_self(project(attended_self, self_out))
    key_cross = project(enc_rows, cross_key).astype(jnp.bfloat16)
    value_cross = project(enc_rows, cross_value).astype(jnp.bfloat16)
    scaled_two, inverse_two = norm_parts(after_self)
    normed_two = (scaled_two * gain_cross).astype(jnp.bfloat16)
    query_cross = project(normed_two, cross_query).astype(jnp.bfloat16)
    attended_cross = run_kernel(
        partial(cross_forward_kernel, slots),
        low_like(query_cross),
        "cross_forward",
        16 * pair_flops,
        query_cross,
        key_cross,
        value_cross,
        slot_rows,
    )
    after_cross = after_self + mix_cross(project(attended_cross, cross_out))
    scaled_three, inverse_three = norm_parts(after_cross)
    normed_three = (scaled_three * gain_ffn).astype(jnp.bfloat16)
    gate_act = project(normed_three, gate_weight)
    up_act = project(normed_three, up_weight)
    activated, glu_pullback = jax.vjp(glu_product, gate_act, up_act)
    inner_act = activated.astype(jnp.bfloat16)
    layer_out = after_cross + mix_ffn(project(inner_act, down_weight))
    grad_low = grad_layer.astype(jnp.bfloat16)
    grad_down = contract_rows(grad_low, inner_act)
    grad_inner = contract_cols(grad_low, down_weight)
    grad_gate, grad_up = glu_pullback(grad_inner)
    gate_low = grad_gate.astype(jnp.bfloat16)
    up_low = grad_up.astype(jnp.bfloat16)
    grad_gate_weight = contract_rows(normed_three, gate_low)
    grad_up_weight = contract_rows(normed_three, up_low)
    grad_normed_three = back_ffn(
        contract_cols(gate_low, gate_weight) + contract_cols(up_low, up_weight)
    )
    grad_gain_ffn = jnp.sum(grad_normed_three * scaled_three, axis=0)
    grad_after_cross = grad_layer + norm_back(
        grad_normed_three, gain_ffn, scaled_three, inverse_three
    )
    ffn_grads = ffn_hook(grad_gate_weight, grad_up_weight, grad_down, grad_gain_ffn)
    cross_low = grad_after_cross.astype(jnp.bfloat16)
    grad_cross_out = contract_rows(cross_low, attended_cross)
    grad_attended = contract_cols(cross_low, cross_out).astype(jnp.bfloat16)
    grad_query, grad_keys, grad_values = run_kernel(
        partial(cross_backward_kernel, slots),
        (low_like(query_cross), low_like(key_cross), low_like(value_cross)),
        "cross_backward",
        32 * pair_flops,
        query_cross,
        key_cross,
        value_cross,
        slot_rows,
        grad_attended,
    )
    grad_cross_query = contract_rows(normed_two, grad_query)
    grad_cross_key = contract_rows(enc_rows, grad_keys)
    grad_cross_value = contract_rows(enc_rows, grad_values)
    grad_normed_two, grad_encoded = back_cross(
        contract_cols(grad_query, cross_query),
        contract_cols(grad_keys, cross_key) + contract_cols(grad_values, cross_value),
    )
    grad_gain_cross = jnp.sum(grad_normed_two * scaled_two, axis=0)
    grad_after_self = grad_after_cross + norm_back(
        grad_normed_two, gain_cross, scaled_two, inverse_two
    )
    self_low = grad_after_self.astype(jnp.bfloat16)
    grad_self_out = contract_rows(self_low, attended_self)
    grad_attended = contract_cols(self_low, self_out).astype(jnp.bfloat16)
    grad_query, grad_keys, grad_values, grad_skew = run_kernel(
        self_backward_kernel,
        (
            low_like(query_self),
            low_like(key_self),
            low_like(value_self),
            jax.ShapeDtypeStruct(skew_table.shape, jnp.float32),
        ),
        "self_backward",
        32 * pair_flops,
        query_self,
        key_self,
        value_self,
        skew_table,
        seg_rows,
        seg_cols,
        grad_attended,
    )
    grad_distance = jnp.roll(grad_skew, 1, axis=1)[:, :span]
    grad_bias = jnp.dot(
        bucket_onehot.T, grad_distance.T, precision=highest, preferred_element_type=jnp.float32
    )
    grad_self_query = contract_rows(normed_one, grad_query)
    grad_self_key = contract_rows(normed_one, grad_keys)
    grad_self_value = contract_rows(normed_one, grad_values)
    grad_normed_one = back_self(
        contract_cols(grad_query, self_query)
        + contract_cols(grad_keys, self_key)
        + contract_cols(grad_values, self_value)
    )
    grad_gain_self = jnp.sum(grad_normed_one * scaled_one, axis=0)
    grad_tokens = grad_after_self + norm_back(grad_normed_one, gain_self, scaled_one, inverse_one)
    attention_grads = (
        grad_gain_self,
        grad_gain_cross,
        grad_self_query,
        grad_self_key,
        grad_self_value,
        grad_self_out,
        grad_bias,
        grad_cross_query,
        grad_cross_key,
        grad_cross_value,
        grad_cross_out,
    )
    return (layer_out, grad_tokens, grad_encoded, ffn_grads, attention_grads)


def local(
    tokens,
    encoded,
    cotangent,
    seq_lengths,
    enc_slot,
    buckets,
    gain_self,
    gain_cross,
    gain_ffn,
    self_query,
    self_key,
    self_value,
    self_out,
    bias_table,
    cross_query,
    cross_key,
    cross_value,
    cross_out,
    gate_weight,
    up_weight,
    down_weight,
):
    row_count = tokens.shape[0]
    slot_count = seq_lengths.shape[0]
    segment, offset, row_slot = layout(seq_lengths, enc_slot, row_count)
    live_all = (segment < slot_count).astype(jnp.float32)[:, None]

    def ffn_hook(grad_gate_weight, grad_up_weight, grad_down, grad_gain_ffn):
        parts = (grad_gate_weight, grad_up_weight, grad_down, grad_gain_ffn)
        return parts

    weights = (
        gain_self,
        gain_cross,
        gain_ffn,
        self_query,
        self_key,
        self_value,
        self_out,
        bias_table,
        cross_query,
        cross_key,
        cross_value,
        cross_out,
        gate_weight,
        up_weight,
        down_weight,
    )
    def sum_tensor(operand):
        return lax.psum(operand.astype(jnp.bfloat16), "tensor").astype(jnp.float32)

    mixers = (
        sum_tensor,
        sum_tensor,
        sum_tensor,
        sum_tensor,
        lambda first, second: (
            sum_tensor(first),
            lax.psum_scatter(
                second.astype(jnp.bfloat16), "tensor", scatter_dimension=1, tiled=True
            ).astype(jnp.float32),
        ),
        sum_tensor,
    )
    layer_full, grad_tokens, grad_encoded, ffn_grads, attention_grads = layer_pass(
        tokens.astype(jnp.float32),
        encoded,
        cotangent.astype(jnp.float32) * live_all,
        segment,
        row_slot,
        slot_count,
        buckets,
        weights,
        mixers,
        ffn_hook,
    )
    layer_out = layer_full * live_all
    (
        grad_gain_self,
        grad_gain_cross,
        grad_self_query,
        grad_self_key,
        grad_self_value,
        grad_self_out,
        grad_bias,
        grad_cross_query,
        grad_cross_key,
        grad_cross_value,
        grad_cross_out,
    ) = attention_grads
    bias_shape = grad_bias.shape
    grad_gate, grad_up, grad_down, grad_gain_ffn = ffn_grads

    def sum_rows(parts):
        joined = jnp.concatenate([part.astype(jnp.bfloat16) for part in parts], axis=1)
        summed = lax.psum_scatter(joined, "dp", scatter_dimension=0, tiled=True).astype(jnp.float32)
        ends = [sum(part.shape[1] for part in parts[: at + 1]) for at in range(len(parts))]
        return jnp.split(summed, ends[:-1], axis=1)

    sum_gate, sum_up, sum_down = sum_rows((grad_gate, grad_up, grad_down))
    sum_cross_query, sum_cross_key, sum_cross_value, sum_cross_out = sum_rows(
        (grad_cross_query, grad_cross_key, grad_cross_value, grad_cross_out)
    )
    sum_query, sum_key, sum_value, sum_out = sum_rows(
        (grad_self_query, grad_self_key, grad_self_value, grad_self_out)
    )
    sum_out, sum_cross_out, sum_down = sum_out.T, sum_cross_out.T, sum_down.T
    small = jnp.concatenate(
        [grad_gain_self, grad_gain_cross, grad_gain_ffn, grad_bias.reshape(-1)]
    )
    sum_gain_self, sum_gain_cross, sum_gain_ffn, sum_bias = jnp.split(
        lax.psum(small, "dp"), [width * grad_gain_self.shape[0] for width in (1, 2, 3)]
    )
    sum_bias = sum_bias.reshape(bias_shape)
    return (
        layer_out.astype(jnp.bfloat16),
        grad_tokens,
        grad_encoded,
        sum_gain_self,
        sum_gain_cross,
        sum_gain_ffn,
        sum_query,
        sum_key,
        sum_value,
        sum_out,
        sum_bias,
        sum_cross_query,
        sum_cross_key,
        sum_cross_value,
        sum_cross_out,
        sum_gate,
        sum_up,
        sum_down,
    )


def solution(mesh):
    placed = (
        P("dp", None),
        P("dp", None),
        P("dp", None),
        P("dp"),
        P("dp"),
        P(),
        P(),
        P(),
        P(),
        P(None, "tensor"),
        P(None, "tensor"),
        P(None, "tensor"),
        P("tensor", None),
        P(None, "tensor"),
        P(None, "tensor"),
        P(None, "tensor"),
        P(None, "tensor"),
        P("tensor", None),
        P(None, "tensor"),
        P(None, "tensor"),
        P("tensor", None),
    )
    return jax.shard_map(
        local,
        mesh=mesh,
        in_specs=placed,
        out_specs=(
            P("dp", None),
            P("dp", None),
            P("dp", "tensor"),
            P(),
            P(),
            P(),
            P("dp", "tensor"),
            P("dp", "tensor"),
            P("dp", "tensor"),
            P("tensor", "dp"),
            P(None, "tensor"),
            P("dp", "tensor"),
            P("dp", "tensor"),
            P("dp", "tensor"),
            P("tensor", "dp"),
            P("dp", "tensor"),
            P("dp", "tensor"),
            P("tensor", "dp"),
        ),
        check_vma=False,
    )
```

```python
from functools import partial

import jax
import jax.numpy as jnp
from jax import lax
from jax.experimental import pallas as pl
from jax.experimental.pallas import tpu as pltpu
from jax.sharding import PartitionSpec as P

HD = 64


eps = 1e-06
masked_score = -1e30
highest = lax.Precision.HIGHEST


def layout(lengths, slots_of, row_count):
    seq_ends = jnp.cumsum(lengths)
    seq_starts = seq_ends - lengths
    where_row = jnp.arange(row_count, dtype=jnp.int32)
    segment = jnp.sum((where_row[:, None] >= seq_ends[None, :]).astype(jnp.int32), axis=1)
    all_starts = jnp.concatenate([seq_starts, seq_ends[-1:]])
    labels = jnp.arange(all_starts.shape[0], dtype=jnp.int32)
    chosen = segment[:, None] == labels[None, :]
    offset = where_row - jnp.sum(jnp.where(chosen, all_starts[None, :], 0), axis=1)
    slot_table = jnp.concatenate([slots_of, jnp.zeros((1,), jnp.int32)])
    row_slot = jnp.sum(jnp.where(chosen, slot_table[None, :], 0), axis=1)
    return (segment, offset, row_slot)


def project(left_side, right_side):
    return jnp.dot(left_side, right_side, preferred_element_type=jnp.float32)


def contract_rows(left_side, right_side):
    return lax.dot_general(
        left_side, right_side, (((0,), (0,)), ((), ())), preferred_element_type=jnp.float32
    )


def contract_cols(left_side, right_side):
    return lax.dot_general(
        left_side, right_side, (((1,), (1,)), ((), ())), preferred_element_type=jnp.float32
    )


def norm_parts(operand):
    inverse = lax.rsqrt(jnp.mean(operand * operand, axis=-1, keepdims=True) + eps)
    return (operand * inverse, inverse)


def norm_back(grad_normed, gain_vector, scaled, inverse):
    grad_scaled = grad_normed * gain_vector
    return inverse * (grad_scaled - scaled * jnp.mean(grad_scaled * scaled, axis=-1, keepdims=True))


def glu_product(gate_act, up_act):
    return jax.nn.gelu(gate_act, approximate=True) * up_act


def dot_nn(left_side, right_side):
    return jnp.dot(left_side, right_side, preferred_element_type=jnp.float32)


def softmax_parts(scores):
    exp_scores = jnp.exp(scores - jnp.max(scores, axis=-1, keepdims=True))
    return exp_scores / jnp.sum(exp_scores, axis=-1, keepdims=True)


def self_weights(q_head, k_head, table_row, allowed):
    rows, cols = allowed.shape
    bias = pltpu.roll(
        jnp.broadcast_to(table_row, (rows, cols)), 0, 1, stride=1, stride_axis=0
    )
    scores = contract_cols(q_head, k_head) + bias
    return softmax_parts(jnp.where(allowed, scores, masked_score))


def self_allowed(seg_rows, seg_cols):
    shape = (seg_rows.shape[0], seg_cols.shape[1])
    row = lax.broadcasted_iota(jnp.int32, shape, 0)
    col = lax.broadcasted_iota(jnp.int32, shape, 1)
    return (seg_rows == seg_cols) & (col <= row)


def self_forward_kernel(q_ref, k_ref, v_ref, table_ref, seg_rows, seg_cols, out_ref):
    allowed = self_allowed(seg_rows[...], seg_cols[...])
    for head in range(q_ref.shape[1] // HD):
        lanes = slice(head * HD, (head + 1) * HD)
        weights = self_weights(
            q_ref[:, lanes], k_ref[:, lanes], table_ref[head : head + 1, :], allowed
        )
        out_ref[:, lanes] = dot_nn(weights.astype(jnp.bfloat16), v_ref[:, lanes]).astype(
            jnp.bfloat16
        )


def score_grads(weights, grad_weights):
    delta_rows = jnp.sum(weights * grad_weights, axis=-1, keepdims=True)
    return (weights * (grad_weights - delta_rows)).astype(jnp.bfloat16)


def self_backward_kernel(
    q_ref, k_ref, v_ref, table_ref, seg_rows, seg_cols, g_ref, dq_ref, dk_ref, dv_ref, skew_ref
):
    allowed = self_allowed(seg_rows[...], seg_cols[...])
    rows, cols = allowed.shape
    flip = (
        lax.broadcasted_iota(jnp.int32, (cols, cols), 0)
        + lax.broadcasted_iota(jnp.int32, (cols, cols), 1)
        == cols - 1
    ).astype(jnp.float32).astype(jnp.bfloat16)
    for head in range(q_ref.shape[1] // HD):
        lanes = slice(head * HD, (head + 1) * HD)
        q_head, k_head, v_head, g_head = (
            q_ref[:, lanes],
            k_ref[:, lanes],
            v_ref[:, lanes],
            g_ref[:, lanes],
        )
        weights = self_weights(q_head, k_head, table_ref[head : head + 1, :], allowed)
        grad_scores = score_grads(weights, contract_cols(g_head, v_head))
        dq_ref[:, lanes] = dot_nn(grad_scores, k_head).astype(jnp.bfloat16)
        dk_ref[:, lanes] = contract_rows(grad_scores, q_head).astype(jnp.bfloat16)
        dv_ref[:, lanes] = contract_rows(weights.astype(jnp.bfloat16), g_head).astype(
            jnp.bfloat16
        )
        skewed = pltpu.roll(dot_nn(grad_scores, flip), 0, 1, stride=1, stride_axis=0)
        skew_ref[head : head + 1, :] = jnp.sum(skewed, axis=0, keepdims=True)


def slot_masked(operand, slot_rows, slot):
    return jnp.where(slot_rows == slot, operand, jnp.zeros_like(operand))


def slot_cols(left_side, right_ref, lanes, slot_rows, slots):
    span = right_ref.shape[0] // slots
    return sum(
        contract_cols(
            slot_masked(left_side, slot_rows, slot),
            right_ref[slot * span : (slot + 1) * span, lanes],
        )
        for slot in range(slots)
    )


def slot_pick(left_side, right_ref, lanes, slot_rows, slots):
    span = right_ref.shape[0] // slots
    return sum(
        slot_masked(
            dot_nn(left_side, right_ref[slot * span : (slot + 1) * span, lanes]), slot_rows, slot
        )
        for slot in range(slots)
    )


def cross_forward_kernel(slots, q_ref, k_ref, v_ref, slot_ref, out_ref):
    slot_rows = slot_ref[...]
    for head in range(q_ref.shape[1] // HD):
        lanes = slice(head * HD, (head + 1) * HD)
        weights = softmax_parts(slot_cols(q_ref[:, lanes], k_ref, lanes, slot_rows, slots))
        out_ref[:, lanes] = slot_pick(
            weights.astype(jnp.bfloat16), v_ref, lanes, slot_rows, slots
        ).astype(jnp.bfloat16)


def cross_backward_kernel(
    slots, q_ref, k_ref, v_ref, slot_ref, g_ref, dq_ref, dk_ref, dv_ref
):
    slot_rows = slot_ref[...]
    span = k_ref.shape[0] // slots
    for head in range(q_ref.shape[1] // HD):
        lanes = slice(head * HD, (head + 1) * HD)
        q_head, g_head = q_ref[:, lanes], g_ref[:, lanes]
        weights = softmax_parts(slot_cols(q_head, k_ref, lanes, slot_rows, slots))
        grad_scores = score_grads(weights, slot_cols(g_head, v_ref, lanes, slot_rows, slots))
        weights_low = weights.astype(jnp.bfloat16)
        dq_ref[:, lanes] = slot_pick(grad_scores, k_ref, lanes, slot_rows, slots).astype(
            jnp.bfloat16
        )
        for slot in range(slots):
            keys = slice(slot * span, (slot + 1) * span)
            dk_ref[keys, lanes] = contract_rows(
                grad_scores, slot_masked(q_head, slot_rows, slot)
            ).astype(jnp.bfloat16)
            dv_ref[keys, lanes] = contract_rows(
                weights_low, slot_masked(g_head, slot_rows, slot)
            ).astype(jnp.bfloat16)


def exchange_kernel(counts, *refs):
    tensor_count, data_count = counts
    if data_count:
        x_ref, w_ref, sum_ref, part_ref = refs[:4]
        inbox, total, send_x, recv_x, send_t, recv_t, w_inbox, send_w, recv_w = refs[4:]
    else:
        x_ref, sum_ref = refs[:2]
        inbox, total, send_x, recv_x, send_t, recv_t = refs[2:]
    me = lax.axis_index("tensor")
    peers = [lax.rem(me + step, tensor_count) for step in range(1, tensor_count)]
    barrier = pltpu.get_barrier_semaphore()
    for peer in peers:
        pl.semaphore_signal(
            barrier, inc=1, device_id={"tensor": peer}, device_id_type=pl.DeviceIdType.MESH
        )
    w_peers = []
    if data_count:
        w_me = lax.axis_index("dp")
        w_peers = [lax.rem(w_me + step, data_count) for step in range(1, data_count)]
        for peer in w_peers:
            pl.semaphore_signal(
                barrier, inc=1, device_id={"dp": peer}, device_id_type=pl.DeviceIdType.MESH
            )
    pl.semaphore_wait(barrier, len(peers) + len(w_peers))

    def send(src, dst, send_sem, recv_sem, device):
        copy = pltpu.make_async_remote_copy(
            src_ref=src,
            dst_ref=dst,
            send_sem=send_sem,
            recv_sem=recv_sem,
            device_id=device,
            device_id_type=pl.DeviceIdType.MESH,
        )
        copy.start()
        return copy

    x_copies = [
        send(x_ref.at[peer], inbox.at[at], send_x.at[at], recv_x.at[at], {"tensor": peer})
        for at, peer in enumerate(peers)
    ]
    w_copies = [
        send(w_ref.at[peer], w_inbox.at[at], send_w.at[at], recv_w.at[at], {"dp": peer})
        for at, peer in enumerate(w_peers)
    ]
    own = x_ref[me].astype(jnp.float32)
    for at, copy in enumerate(x_copies):
        copy.wait()
        own = own + inbox[at].astype(jnp.float32)
    total[me] = own.astype(jnp.bfloat16)
    t_copies = [
        send(total.at[me], total.at[me], send_t.at[at], recv_t.at[at], {"tensor": peer})
        for at, peer in enumerate(peers)
    ]
    if data_count:
        for copy in w_copies:
            copy.wait()
        part = w_ref[w_me].astype(jnp.float32)
        for at in range(len(w_copies)):
            part = part + w_inbox[at].astype(jnp.float32)
        part_ref[...] = part
    for copy in t_copies:
        copy.wait()
    sum_ref[...] = total[...]


def exchange(operand, parts, collective_id):
    tensor_count, data_count = lax.axis_size("tensor"), lax.axis_size("dp")
    rows, width = operand.shape
    shared = (tensor_count, rows // tensor_count, width)
    joined = None
    if parts:
        joined = jnp.concatenate([part.astype(jnp.bfloat16) for part in parts], axis=1)
    inside = data_count if parts and data_count <= 8 else 0
    dma = pltpu.SemaphoreType.DMA
    whole = pl.BlockSpec(memory_space=pltpu.VMEM)
    operands = [operand.astype(jnp.bfloat16).reshape(shared)]
    outs = [jax.ShapeDtypeStruct(shared, jnp.bfloat16)]
    scratch = [
        pltpu.VMEM((tensor_count - 1,) + shared[1:], jnp.bfloat16),
        pltpu.VMEM(shared, jnp.bfloat16),
    ] + [dma((tensor_count - 1,))] * 4
    if inside:
        block = (joined.shape[0] // inside, joined.shape[1])
        operands.append(joined.reshape((inside,) + block))
        outs.append(jax.ShapeDtypeStruct(block, jnp.float32))
        scratch += [pltpu.VMEM((inside - 1,) + block, jnp.bfloat16)] + [dma((inside - 1,))] * 2
    result = pl.pallas_call(
        partial(exchange_kernel, (tensor_count, inside)),
        out_shape=outs,
        in_specs=[whole] * len(operands),
        out_specs=[whole] * len(outs),
        scratch_shapes=scratch,
        compiler_params=pltpu.CompilerParams(
            collective_id=collective_id,
            has_side_effects=True,
            vmem_limit_bytes=48 * 1024 * 1024,
        ),
        cost_estimate=pl.CostEstimate(flops=1 << 34, bytes_accessed=1 << 26, transcendentals=0),
        name=f"exchange_{collective_id}",
    )(*operands)
    summed = result[0].reshape(rows, width).astype(jnp.float32)
    if not parts:
        return summed
    if inside:
        scattered = result[1]
    else:
        scattered = lax.psum_scatter(joined, "dp", scatter_dimension=0, tiled=True).astype(
            jnp.float32
        )
    ends = [sum(part.shape[1] for part in parts[: at + 1]) for at in range(len(parts))]
    return summed, jnp.split(scattered, ends[:-1], axis=1)


def run_kernel(body, outs, name, flops, *operands):
    whole = pl.BlockSpec(memory_space=pltpu.VMEM)
    return pl.pallas_call(
        body,
        out_shape=outs,
        in_specs=[whole] * len(operands),
        out_specs=jax.tree.map(lambda leaf: whole, outs),
        compiler_params=pltpu.CompilerParams(vmem_limit_bytes=48 * 1024 * 1024),
        cost_estimate=pl.CostEstimate(flops=flops, bytes_accessed=1 << 22, transcendentals=0),
        name=name,
    )(*operands)


def layer_pass(
    hidden_in,
    enc_rows,
    grad_layer,
    segment,
    row_slot,
    slots,
    buckets,
    weights,
    mixers,
):
    (
        gain_self,
        gain_cross,
        gain_ffn,
        self_query,
        self_key,
        self_value,
        self_out,
        bias_table,
        cross_query,
        cross_key,
        cross_value,
        cross_out,
        gate_weight,
        up_weight,
        down_weight,
    ) = weights
    mix_ffn, scatter_encoded = mixers
    row_count = hidden_in.shape[0]
    span = buckets.shape[0]
    bias_values = bias_table.astype(jnp.float32)
    bucket_labels = jnp.arange(bias_values.shape[0], dtype=jnp.int32)
    bucket_onehot = (buckets[:, None] == bucket_labels[None, :]).astype(jnp.float32)
    distance_table = jnp.dot(
        bucket_onehot, bias_values, precision=highest, preferred_element_type=jnp.float32
    ).T
    back = lax.rem(row_count - jnp.arange(row_count, dtype=jnp.int32), row_count)
    skew_onehot = (back[:, None] == jnp.arange(span, dtype=jnp.int32)[None, :]).astype(jnp.float32)
    skew_table = jnp.dot(
        distance_table, skew_onehot.T, precision=highest, preferred_element_type=jnp.float32
    )
    seg_rows, seg_cols = segment[:, None], segment[None, :]
    slot_rows = row_slot[:, None]

    scaled_one, inverse_one = norm_parts(hidden_in)
    normed_one = (scaled_one * gain_self).astype(jnp.bfloat16)
    query_self = project(normed_one, self_query).astype(jnp.bfloat16)
    key_self = project(normed_one, self_key).astype(jnp.bfloat16)
    value_self = project(normed_one, self_value).astype(jnp.bfloat16)
    low_like = lambda operand: jax.ShapeDtypeStruct(operand.shape, jnp.bfloat16)
    pair_flops = 2 * row_count * row_count * self_query.shape[1]
    attended_self = run_kernel(
        self_forward_kernel,
        low_like(query_self),
        "self_forward",
        8 * pair_flops,
        query_self,
        key_self,
        value_self,
        skew_table,
        seg_rows,
        seg_cols,
    )
    after_self = hidden_in + exchange(project(attended_self, self_out), (), 0)
    key_cross = project(enc_rows, cross_key).astype(jnp.bfloat16)
    value_cross = project(enc_rows, cross_value).astype(jnp.bfloat16)
    scaled_two, inverse_two = norm_parts(after_self)
    normed_two = (scaled_two * gain_cross).astype(jnp.bfloat16)
    query_cross = project(normed_two, cross_query).astype(jnp.bfloat16)
    attended_cross = run_kernel(
        partial(cross_forward_kernel, slots),
        low_like(query_cross),
        "cross_forward",
        16 * pair_flops,
        query_cross,
        key_cross,
        value_cross,
        slot_rows,
    )
    after_cross = after_self + exchange(project(attended_cross, cross_out), (), 0)
    scaled_three, inverse_three = norm_parts(after_cross)
    normed_three = (scaled_three * gain_ffn).astype(jnp.bfloat16)
    gate_act = project(normed_three, gate_weight)
    up_act = project(normed_three, up_weight)
    activated, glu_pullback = jax.vjp(glu_product, gate_act, up_act)
    inner_act = activated.astype(jnp.bfloat16)
    layer_out = after_cross + mix_ffn(project(inner_act, down_weight))
    grad_low = grad_layer.astype(jnp.bfloat16)
    grad_down = contract_rows(grad_low, inner_act)
    grad_inner = contract_cols(grad_low, down_weight)
    grad_gate, grad_up = glu_pullback(grad_inner)
    gate_low = grad_gate.astype(jnp.bfloat16)
    up_low = grad_up.astype(jnp.bfloat16)
    grad_gate_weight = contract_rows(normed_three, gate_low)
    grad_up_weight = contract_rows(normed_three, up_low)
    grad_normed_three, ffn_grads = exchange(
        contract_cols(gate_low, gate_weight) + contract_cols(up_low, up_weight),
        (grad_gate_weight, grad_up_weight, grad_down),
        1,
    )
    grad_gain_ffn = jnp.sum(grad_normed_three * scaled_three, axis=0)
    grad_after_cross = grad_layer + norm_back(
        grad_normed_three, gain_ffn, scaled_three, inverse_three
    )
    cross_low = grad_after_cross.astype(jnp.bfloat16)
    grad_cross_out = contract_rows(cross_low, attended_cross)
    grad_attended = contract_cols(cross_low, cross_out).astype(jnp.bfloat16)
    grad_query, grad_keys, grad_values = run_kernel(
        partial(cross_backward_kernel, slots),
        (low_like(query_cross), low_like(key_cross), low_like(value_cross)),
        "cross_backward",
        32 * pair_flops,
        query_cross,
        key_cross,
        value_cross,
        slot_rows,
        grad_attended,
    )
    grad_cross_query = contract_rows(normed_two, grad_query)
    grad_cross_key = contract_rows(enc_rows, grad_keys)
    grad_cross_value = contract_rows(enc_rows, grad_values)
    grad_encoded = scatter_encoded(
        contract_cols(grad_keys, cross_key) + contract_cols(grad_values, cross_value)
    )
    grad_normed_two, cross_grads = exchange(
        contract_cols(grad_query, cross_query),
        (grad_cross_query, grad_cross_key, grad_cross_value, grad_cross_out),
        2,
    )
    grad_gain_cross = jnp.sum(grad_normed_two * scaled_two, axis=0)
    grad_after_self = grad_after_cross + norm_back(
        grad_normed_two, gain_cross, scaled_two, inverse_two
    )
    self_low = grad_after_self.astype(jnp.bfloat16)
    grad_self_out = contract_rows(self_low, attended_self)
    grad_attended = contract_cols(self_low, self_out).astype(jnp.bfloat16)
    grad_query, grad_keys, grad_values, grad_skew = run_kernel(
        self_backward_kernel,
        (
            low_like(query_self),
            low_like(key_self),
            low_like(value_self),
            jax.ShapeDtypeStruct(skew_table.shape, jnp.float32),
        ),
        "self_backward",
        32 * pair_flops,
        query_self,
        key_self,
        value_self,
        skew_table,
        seg_rows,
        seg_cols,
        grad_attended,
    )
    grad_distance = jnp.roll(grad_skew, 1, axis=1)[:, :span]
    grad_bias = jnp.dot(
        bucket_onehot.T, grad_distance.T, precision=highest, preferred_element_type=jnp.float32
    )
    grad_self_query = contract_rows(normed_one, grad_query)
    grad_self_key = contract_rows(normed_one, grad_keys)
    grad_self_value = contract_rows(normed_one, grad_values)
    partial_normed_one = (
        contract_cols(grad_query, self_query)
        + contract_cols(grad_keys, self_key)
        + contract_cols(grad_values, self_value)
    )
    share_gain_self = jnp.sum(partial_normed_one * scaled_one, axis=0)
    grad_normed_one, self_grads = exchange(
        partial_normed_one,
        (grad_self_query, grad_self_key, grad_self_value, grad_self_out),
        3,
    )
    grad_tokens = grad_after_self + norm_back(grad_normed_one, gain_self, scaled_one, inverse_one)
    small_grads = (share_gain_self, grad_gain_cross, grad_gain_ffn, grad_bias)
    return (layer_out, grad_tokens, grad_encoded, ffn_grads, cross_grads, self_grads, small_grads)


def local(
    tokens,
    encoded,
    cotangent,
    seq_lengths,
    enc_slot,
    buckets,
    gain_self,
    gain_cross,
    gain_ffn,
    self_query,
    self_key,
    self_value,
    self_out,
    bias_table,
    cross_query,
    cross_key,
    cross_value,
    cross_out,
    gate_weight,
    up_weight,
    down_weight,
):
    row_count = tokens.shape[0]
    slot_count = seq_lengths.shape[0]
    segment, offset, row_slot = layout(seq_lengths, enc_slot, row_count)
    live_all = (segment < slot_count).astype(jnp.float32)[:, None]

    weights = (
        gain_self,
        gain_cross,
        gain_ffn,
        self_query,
        self_key,
        self_value,
        self_out,
        bias_table,
        cross_query,
        cross_key,
        cross_value,
        cross_out,
        gate_weight,
        up_weight,
        down_weight,
    )
    mixers = (
        lambda operand: lax.psum(operand.astype(jnp.bfloat16), "tensor").astype(jnp.float32),
        lambda operand: lax.psum_scatter(
            operand.astype(jnp.bfloat16), "tensor", scatter_dimension=1, tiled=True
        ).astype(jnp.float32),
    )
    layer_full, grad_tokens, grad_encoded, ffn_grads, cross_grads, self_grads, small_grads = layer_pass(
        tokens.astype(jnp.float32),
        encoded,
        cotangent.astype(jnp.float32) * live_all,
        segment,
        row_slot,
        slot_count,
        buckets,
        weights,
        mixers,
    )
    layer_out = layer_full * live_all
    sum_gate, sum_up, sum_down = ffn_grads
    sum_cross_query, sum_cross_key, sum_cross_value, sum_cross_out = cross_grads
    sum_query, sum_key, sum_value, sum_out = self_grads
    sum_out, sum_cross_out, sum_down = sum_out.T, sum_cross_out.T, sum_down.T
    share_gain_self, grad_gain_cross, grad_gain_ffn, grad_bias = small_grads
    bias_shape = grad_bias.shape
    tensor_at = lax.axis_index("tensor")
    once = (tensor_at == 0).astype(jnp.float32)
    bias_rows = jnp.arange(lax.axis_size("tensor"))[:, None] == tensor_at
    small = jnp.concatenate(
        [
            share_gain_self,
            once * grad_gain_cross,
            once * grad_gain_ffn,
            jnp.where(bias_rows, grad_bias.reshape(1, -1), 0.0).reshape(-1),
        ]
    )
    sum_gain_self, sum_gain_cross, sum_gain_ffn, sum_bias = jnp.split(
        lax.psum(small, ("dp", "tensor")),
        [width * share_gain_self.shape[0] for width in (1, 2, 3)],
    )
    sum_bias = sum_bias.reshape(bias_rows.shape[0], -1)
    sum_bias = jnp.sum(jnp.where(bias_rows, sum_bias, 0.0), axis=0).reshape(bias_shape)
    return (
        layer_out.astype(jnp.bfloat16),
        grad_tokens,
        grad_encoded,
        sum_gain_self,
        sum_gain_cross,
        sum_gain_ffn,
        sum_query,
        sum_key,
        sum_value,
        sum_out,
        sum_bias,
        sum_cross_query,
        sum_cross_key,
        sum_cross_value,
        sum_cross_out,
        sum_gate,
        sum_up,
        sum_down,
    )


def solution(mesh):
    placed = (
        P("dp", None),
        P("dp", None),
        P("dp", None),
        P("dp"),
        P("dp"),
        P(),
        P(),
        P(),
        P(),
        P(None, "tensor"),
        P(None, "tensor"),
        P(None, "tensor"),
        P("tensor", None),
        P(None, "tensor"),
        P(None, "tensor"),
        P(None, "tensor"),
        P(None, "tensor"),
        P("tensor", None),
        P(None, "tensor"),
        P(None, "tensor"),
        P("tensor", None),
    )
    return jax.shard_map(
        local,
        mesh=mesh,
        in_specs=placed,
        out_specs=(
            P("dp", None),
            P("dp", None),
            P("dp", "tensor"),
            P(),
            P(),
            P(),
            P("dp", "tensor"),
            P("dp", "tensor"),
            P("dp", "tensor"),
            P("tensor", "dp"),
            P(None, "tensor"),
            P("dp", "tensor"),
            P("dp", "tensor"),
            P("dp", "tensor"),
            P("tensor", "dp"),
            P("dp", "tensor"),
            P("dp", "tensor"),
            P("tensor", "dp"),
        ),
        check_vma=False,
    )
```
